32 devices in a mesh: dp: 8 (over z, x), row: 2 (over core), col: 2 (over y).
Axes of the slice: x: 2, y: 2, z: 4, core: 2. Of those that a mesh axis runs over, the one named last changes fastest.
Arguments:
- tokens: bfloat16 [128, 197, 768], P(('dp', 'row', 'col')), may hold values from -6 to 6
- cotangent: bfloat16 [128, 197, 768], P(('dp', 'row', 'col')), may hold values from -6 to 6
- triple_weight: bfloat16 [768, 3, 768], P('row', None, 'col'), may hold values from -0.3125 to 0.3125
- attend_bias: float32 [2, 768], P(None, 'col'), may hold values from -2 to 2
- merge_weight: bfloat16 [768, 768], P('col', 'row'), may hold values from -1.25 to 1.25
- expand_weight: bfloat16 [768, 3072], P('row', 'col'), may hold values from -0.21875 to 0.21875
- expand_bias: float32 [3072], P('col'), may hold values from -2 to 2
- shrink_weight: bfloat16 [3072, 768], P('col', 'row'), may hold values from -0.15625 to 0.15625
- norm_gain: float32 [2, 768], replicated, may hold values from 0.5 to 1.5
- norm_shift: float32 [2, 768], replicated, may hold values from -2 to 2
- branch_bias: float32 [2, 768], replicated, may hold values from -2 to 2
Outputs:
- block_out: bfloat16 [128, 197, 768], P(('dp', 'row', 'col'))
- tokens_grad: float32 [128, 197, 768], P(('dp', 'row', 'col'))
- triple_grad: float32 [768, 3, 768], P('row', None, 'col')
- attend_grad: float32 [2, 768], P(None, 'col')
- merge_grad: float32 [768, 768], P('col', 'row')
- expand_grad: float32 [768, 3072], P('row', 'col')
- hidden_grad: float32 [3072], P('col')
- shrink_grad: float32 [3072, 768], P('col', 'row')
- gain_grad: float32 [2, 768], replicated
- shift_grad: float32 [2, 768], replicated
- branch_grad: float32 [2, 768], replicated
The draws below stay inside these ranges and needn't reach their ends.
All inputs are finite; a program needn't handle non-finite values.
Results may differ from the reference program's by a relative error of at most 0.012.
The reference program's roundings to bfloat16 on the way (of `normed_one`, `attended`, `normed_two` and `active`) count: a program that leaves them out, or rounds other values in their place, can miss the bound.
Values may be sent and summed in bfloat16 or wider, within the bound.
A program may use at most 128 MiB of HBM per device.

```python
import jax
import jax.numpy as jnp
from jax import lax

D = 768
HEADS = 12
FF = 3072
HEAD_DIM = 64
SEQ = 197
IMAGES = 128


def steps_of(key, extent, cuts, low, top_value):
    level = 1.0
    for axis_at, shards_of in cuts:
        heights = jax.random.uniform(jax.random.fold_in(jax.random.fold_in(key, 6), axis_at), (shards_of,), jnp.float32, low / len(cuts), top_value / len(cuts))
        level = level * jnp.repeat(jnp.exp(heights), extent[axis_at] // shards_of).reshape((-1,) + (1,) * (len(extent) - 1 - axis_at))
    return level


def centred(stream_key, shape, deviation, reach, shards=(), held_as=jnp.bfloat16):
    values = jax.random.normal(stream_key, shape, jnp.float32) * deviation
    if len(shards) > 0:
        values = steps_of(stream_key, shape, shards, -0.22, 0.18) * values
    return jnp.clip(values, min=-reach, max=reach).astype(held_as)


def setup_inputs(seed: int = 0) -> dict:
    seeds = jax.random.split(jax.random.key(seed), 12)
    return {
        "tokens": centred(seeds[0], (IMAGES, SEQ, D), 1.0, 6.0, ((0, 32),)),
        "cotangent": centred(seeds[1], (IMAGES, SEQ, D), 1.0, 6.0, ((0, 32),)),
        "triple_weight": centred(seeds[2], (D, 3, D), (D // 2) ** -0.5, 0.3125, ((0, 2), (2, 2))),
        "attend_bias": centred(seeds[3], (2, D), 0.3, 2.0, ((1, 2),), jnp.float32),
        "merge_weight": centred(seeds[4], (D, D), (D // 32) ** -0.5, 1.25, ((0, 2), (1, 2))),
        "expand_weight": centred(seeds[5], (D, FF), D ** -0.5, 0.21875, ((0, 2), (1, 2))),
        "expand_bias": centred(seeds[6], (FF,), 0.3, 2.0, ((0, 2),), jnp.float32),
        "shrink_weight": centred(seeds[7], (FF, D), (FF // 2) ** -0.5, 0.15625, ((0, 2), (1, 2))),
        "norm_gain": jnp.clip(1.0 + 0.1 * jax.random.normal(seeds[8], (2, D), jnp.float32), 0.5, 1.5),
        "norm_shift": centred(seeds[9], (2, D), 0.3, 2.0, (), jnp.float32),
        "branch_bias": centred(seeds[10], (2, D), 0.3, 2.0, (), jnp.float32),
    }


HIGHEST = lax.Precision.HIGHEST
EPSILON = 1e-06

@jax.custom_vjp
def low(v):
    return lax.optimization_barrier(v.astype(jnp.bfloat16)).astype(jnp.float32)

@jax.custom_vjp
def low_back(v):
    return v

def low_keep(v):
    return (low(v), None)

def low_pass(kept, grad):
    return (grad,)

def back_keep(v):
    return (v, None)

def back_low(kept, grad):
    return (low(grad),)
low.defvjp(low_keep, low_pass)
low_back.defvjp(back_keep, back_low)

def layer_norm(source, norm_scale, norm_offset):
    average = lax.optimization_barrier(jnp.mean(source, axis=-1, keepdims=True))
    variance = lax.optimization_barrier(jnp.mean(source * source, axis=-1, keepdims=True)) - average * average
    return (source - average) * lax.rsqrt(variance + EPSILON) * norm_scale + norm_offset

def to_heads(source):
    return source.reshape(source.shape[0], source.shape[1], HEADS, HEAD_DIM)

def forward(params, inputs):
    triple_weight, attend_bias, merge_weight, expand_weight, expand_bias, shrink_weight, norm_gain, norm_shift, branch_bias = params
    normed_one = low(layer_norm(inputs, norm_gain[0], norm_shift[0]))
    projected = jnp.einsum('nsd,dte->nste', normed_one, triple_weight, precision=HIGHEST)
    queries = to_heads(low(low_back(projected[:, :, 0] + attend_bias[0])))
    key_rows = to_heads(low(low_back(projected[:, :, 1])))
    value_rows = to_heads(low(low_back(projected[:, :, 2] + attend_bias[1])))
    logits = low_back(jnp.einsum('nqhe,nkhe->nhqk', queries, key_rows, precision=HIGHEST)) * HEAD_DIM ** (-0.5)
    log_total = jax.nn.logsumexp(logits, axis=-1, keepdims=True)
    weights = low(jnp.exp(logits - log_total))
    attended = jnp.einsum('nhqk,nkhe->nqhe', weights, value_rows, precision=HIGHEST)
    attended = low(low_back(attended.reshape(inputs.shape[0], inputs.shape[1], HEADS * HEAD_DIM)))
    branch_one = low_back(jnp.einsum('nse,ed->nsd', attended, merge_weight, precision=HIGHEST))
    middle = inputs + branch_one + branch_bias[0]
    normed_two = low(layer_norm(middle, norm_gain[1], norm_shift[1]))
    hidden = low_back(jnp.einsum('nsd,df->nsf', normed_two, expand_weight, precision=HIGHEST) + expand_bias)
    active = low(jax.nn.gelu(hidden, approximate=False))
    branch_two = low_back(jnp.einsum('nsf,fd->nsd', active, shrink_weight, precision=HIGHEST))
    return middle + branch_two + branch_bias[1]

def reference(tokens, cotangent, triple_weight, attend_bias, merge_weight, expand_weight, expand_bias, shrink_weight, norm_gain, norm_shift, branch_bias):
    params = tuple((tensor.astype(jnp.float32) for tensor in (triple_weight, attend_bias, merge_weight, expand_weight, expand_bias, shrink_weight, norm_gain, norm_shift, branch_bias)))
    group_size = 16
    groups = IMAGES // group_size
    inputs = tokens.astype(jnp.float32).reshape(groups, group_size, SEQ, D)
    cotangents = cotangent.astype(jnp.float32).reshape(groups, group_size, SEQ, D)

    def one_group(running, pieces):
        group_inputs, group_cotangents = pieces
        output, pullback = jax.vjp(forward, params, group_inputs)
        param_grads, input_grads = pullback(group_cotangents)
        return (jax.tree.map(jnp.add, running, param_grads), (output.astype(jnp.bfloat16), input_grads))
    initial = jax.tree.map(jnp.zeros_like, params)
    totals, (outputs, input_grads) = lax.scan(one_group, initial, (inputs, cotangents))
    return (outputs.reshape(IMAGES, SEQ, D), input_grads.reshape(IMAGES, SEQ, D), totals[0], totals[1], totals[2], totals[3], totals[4], totals[5], totals[6], totals[7], totals[8])
```

```python
import functools
import math

import jax
import jax.numpy as jnp
from jax import lax
from jax.experimental import pallas as pl
from jax.experimental.pallas import tpu as pltpu
from jax.sharding import PartitionSpec as P

HEAD_DIM = 64
EPSILON = 1e-06
F32 = jnp.float32
BF16 = jnp.bfloat16
VMEM_BYTES = 56 * 1024 * 1024


def mean_rows(source):
    return jnp.mean(source, axis=-1, keepdims=True)


def unit_norm(source):
    average = mean_rows(source)
    variance = mean_rows(source * source) - average * average
    inverse = lax.rsqrt(variance + EPSILON)
    return (source - average) * inverse, inverse


def norm_backward(grad, unit, inverse, gain):
    scaled = grad * gain
    return inverse * (scaled - mean_rows(scaled) - unit * mean_rows(scaled * unit))


def dot(left, right):
    return jnp.dot(left, right, preferred_element_type=F32)


def dot_rows(left, right):
    return lax.dot_general(left, right, (((1,), (1,)), ((), ())), preferred_element_type=F32)


def dot_tokens(left, right):
    return lax.dot_general(left, right, (((0,), (0,)), ((), ())), preferred_element_type=F32)


def column_sum(source):
    return jnp.sum(source, axis=0, keepdims=True)


def assemble_triple(blocks_ref, full_ref, width):
    row_count, col_count, _, depth, cols = blocks_ref.shape
    for r in range(row_count):
        for c in range(col_count):
            for t in range(3):
                full_ref[r * depth : (r + 1) * depth, t * width + c * cols : t * width + (c + 1) * cols] = (
                    blocks_ref[r, c, t]
                )


def assemble_merge(blocks_ref, full_ref):
    row_count, col_count, depth, cols = blocks_ref.shape
    for r in range(row_count):
        for c in range(col_count):
            full_ref[c * depth : (c + 1) * depth, r * cols : (r + 1) * cols] = blocks_ref[r, c]


def attend_kernel(seq, x_ref, triple_ref, merge_ref, vec_ref, qkv_ref, attended_ref, middle_ref, triple_full, merge_full):
    width = x_ref.shape[-1]
    rows = x_ref.shape[1]

    @pl.when(pl.program_id(0) == 0)
    def _():
        assemble_triple(triple_ref, triple_full, width)
        assemble_merge(merge_ref, merge_full)

    x = x_ref[0].astype(F32)
    unit, _ = unit_norm(x)
    normed = (unit * vec_ref[0:1] + vec_ref[1:2]).astype(BF16)
    qkv_ref[0, :, 0:width] = (dot(normed, triple_full[:, 0:width]) + vec_ref[3:4]).astype(BF16)
    qkv_ref[0, :, width : 2 * width] = dot(normed, triple_full[:, width : 2 * width]).astype(BF16)
    qkv_ref[0, :, 2 * width : 3 * width] = (
        dot(normed, triple_full[:, 2 * width : 3 * width]) + vec_ref[4:5]
    ).astype(BF16)
    pair = 2 * HEAD_DIM
    first = lax.broadcasted_iota(jnp.int32, (rows, pair), 1) < HEAD_DIM
    live = lax.broadcasted_iota(jnp.int32, (rows, rows), 1) < seq
    scale = HEAD_DIM**-0.5
    zero = jnp.zeros((rows, pair), BF16)
    for p in range(width // pair):
        q = qkv_ref[0, :, p * pair : (p + 1) * pair]
        k = qkv_ref[0, :, width + p * pair : width + (p + 1) * pair]
        v = qkv_ref[0, :, 2 * width + p * pair : 2 * width + (p + 1) * pair]
        outs = []
        for h in range(2):
            mine = first if h == 0 else jnp.logical_not(first)
            logits = dot_rows(jnp.where(mine, q, zero), k) * scale
            logits = jnp.where(live, logits, -1e30)
            top = jnp.max(logits, axis=-1, keepdims=True)
            powers = jnp.exp(logits - top)
            probs = powers * (1.0 / jnp.sum(powers, axis=-1, keepdims=True))
            outs.append(dot(probs.astype(BF16), v))
        attended_ref[0, :, p * pair : (p + 1) * pair] = jnp.where(first, outs[0], outs[1]).astype(BF16)
    middle_ref[0] = x + dot(attended_ref[0], merge_full[...]) + vec_ref[2:3]


def mlp_kernel(
    middle_ref, g_ref, expand_ref, bias_ref, shrink_ref, vec_ref,
    out_ref, dmid_ref, dexpand_ref, dbias_ref, dshrink_ref, sums_ref,
    normed_ref, acc_ref, back_ref,
):
    step = pl.program_id(0)

    @pl.when(step == 0)
    def _():
        unit, _ = unit_norm(middle_ref[...])
        normed_ref[...] = (unit * vec_ref[0:1] + vec_ref[1:2]).astype(BF16)
        acc_ref[...] = jnp.zeros_like(acc_ref)
        back_ref[...] = jnp.zeros_like(back_ref)

    row_count, _, depth, chunk = expand_ref.shape
    expand = expand_ref[...].reshape(row_count * depth, chunk)
    shrink = jnp.concatenate([shrink_ref[r, 0] for r in range(row_count)], axis=-1)
    normed = normed_ref[...]
    g = g_ref[...]
    hidden = dot(normed, expand) + bias_ref[...]
    cdf = 0.5 * (1.0 + lax.erf(hidden * (0.5**0.5)))
    slope = cdf + hidden * (jnp.exp(-0.5 * hidden * hidden) * (1.0 / math.sqrt(2.0 * math.pi)))
    active = (hidden * cdf).astype(BF16)
    acc_ref[...] += dot(active, shrink)
    dhidden_wide = dot_rows(g, shrink) * slope
    dhidden = dhidden_wide.astype(BF16)
    dbias_ref[...] = column_sum(dhidden.astype(F32))
    back_ref[...] += dot_rows(dhidden, expand)
    dshrink = dot_tokens(active, g).astype(BF16)
    cols = dshrink.shape[1] // row_count
    for r in range(row_count):
        dshrink_ref[r, 0] = dshrink[:, r * cols : (r + 1) * cols]
    dexpand_ref[...] = dot_tokens(normed, dhidden).astype(BF16).reshape(row_count, 1, depth, chunk)

    @pl.when(step == pl.num_programs(0) - 1)
    def _():
        middle = middle_ref[...]
        out_ref[...] = (middle + acc_ref[...] + vec_ref[2:3]).astype(BF16)
        unit, inverse = unit_norm(middle)
        wide = g_ref[...].astype(F32)
        back = back_ref[...]
        dmid = wide + norm_backward(back, unit, inverse, vec_ref[0:1])
        dmid_ref[...] = dmid
        sums_ref[0:1] = column_sum(back * unit)
        sums_ref[1:2] = column_sum(back)
        sums_ref[2:3] = column_sum(dmid)
        sums_ref[3:4] = column_sum(wide)


def back_kernel(
    seq, x_ref, dmid_ref, attended_ref, qkv_ref, triple_ref, merge_ref, vec_ref,
    dx_ref, dtriple_ref, dmerge_ref, sums_ref,
    triple_full, merge_full, dqkv_ref, normed_ref, g1_ref, datt_ref,
):
    images, rows, width = x_ref.shape
    assemble_triple(triple_ref, triple_full, width)
    assemble_merge(merge_ref, merge_full)
    pair = 2 * HEAD_DIM
    scale = HEAD_DIM**-0.5
    sums_ref[...] = jnp.zeros_like(sums_ref)

    @pl.loop(0, images)
    def _(image):
        at = pl.ds(pl.multiple_of(image * rows, 16), rows)
        x = x_ref[image].astype(F32)
        unit, inverse = unit_norm(x)
        normed_ref[at, :] = (unit * vec_ref[0:1] + vec_ref[1:2]).astype(BF16)
        dmid = dmid_ref[image]
        g1 = dmid.astype(BF16)
        g1_ref[at, :] = g1
        datt_ref[...] = dot_rows(g1, merge_full[...]).astype(BF16)
        first = lax.broadcasted_iota(jnp.int32, (rows, pair), 1) < HEAD_DIM
        live = lax.broadcasted_iota(jnp.int32, (rows, rows), 0) < seq
        zero = jnp.zeros((rows, pair), BF16)
        for p in range(width // pair):
            q = qkv_ref[image, :, p * pair : (p + 1) * pair]
            k = qkv_ref[image, :, width + p * pair : width + (p + 1) * pair]
            v = qkv_ref[image, :, 2 * width + p * pair : 2 * width + (p + 1) * pair]
            da = datt_ref[:, p * pair : (p + 1) * pair]
            dq, dk, dv = [], [], []
            for h in range(2):
                mine = first if h == 0 else jnp.logical_not(first)
                logits = dot_rows(k, jnp.where(mine, q, zero)) * scale
                logits = jnp.where(live, logits, -1e30)
                top = jnp.max(logits, axis=0, keepdims=True)
                powers = jnp.exp(logits - top)
                probs = powers * (1.0 / column_sum(powers))
                dprobs = dot_rows(v, jnp.where(mine, da, zero))
                weighted = probs * dprobs
                dlogits = ((weighted - probs * column_sum(weighted)) * scale).astype(BF16)
                dq.append(dot_tokens(dlogits, k))
                dk.append(dot(dlogits, q))
                dv.append(dot(probs.astype(BF16), da))
            for t, parts in enumerate((dq, dk, dv)):
                dqkv_ref[at, t * width + p * pair : t * width + (p + 1) * pair] = jnp.where(
                    first, parts[0], parts[1]
                ).astype(BF16)
        dnormed = dot_rows(dqkv_ref[at, :], triple_full[...])
        dx_ref[image] = dmid + norm_backward(dnormed, unit, inverse, vec_ref[0:1])
        sums_ref[0:1] += column_sum(dnormed * unit)
        sums_ref[1:2] += column_sum(dnormed)
        sums_ref[2:3] += column_sum(dqkv_ref[at, 0:width].astype(F32))
        sums_ref[3:4] += column_sum(dqkv_ref[at, 2 * width : 3 * width].astype(F32))

    row_count, col_count, _, depth, cols = dtriple_ref.shape
    for c in range(col_count):

        @pl.loop(0, 3)
        def _(t):
            at = pl.ds(pl.multiple_of(t * width + c * cols, 128), cols)
            part = dot_tokens(normed_ref[...], dqkv_ref[:, at]).astype(BF16)
            for r in range(row_count):
                dtriple_ref[r, c, t] = part[r * depth : (r + 1) * depth]

    attended = attended_ref[...].reshape(images * rows, width)
    for r in range(row_count):
        part = dot_tokens(attended, g1_ref[:, r * cols : (r + 1) * cols]).astype(BF16)
        for c in range(col_count):
            dmerge_ref[r, c] = part[c * depth : (c + 1) * depth]


def whole(shape):
    return pl.BlockSpec(shape, lambda *_: (0,) * len(shape))


def per_image(shape):
    return pl.BlockSpec((1,) + shape, lambda i: (i, 0, 0))


def params():
    return pltpu.CompilerParams(vmem_limit_bytes=VMEM_BYTES)


def attend(x, triple, merge, vec, seq):
    images, rows, width = x.shape
    return pl.pallas_call(
        functools.partial(attend_kernel, seq),
        grid=(images,),
        in_specs=[per_image((rows, width)), whole(triple.shape), whole(merge.shape), whole(vec.shape)],
        out_specs=[per_image((rows, 3 * width)), per_image((rows, width)), per_image((rows, width))],
        out_shape=[
            jax.ShapeDtypeStruct((images, rows, 3 * width), BF16),
            jax.ShapeDtypeStruct((images, rows, width), BF16),
            jax.ShapeDtypeStruct((images, rows, width), F32),
        ],
        scratch_shapes=[pltpu.VMEM((width, 3 * width), BF16), pltpu.VMEM((width, width), BF16)],
        compiler_params=params(),
        name="attend",
    )(x, triple, merge, vec)


def mlp(middle, g, expand, bias, shrink, vec, chunk):
    tokens, width = middle.shape
    row_count, col_count, depth, units = expand.shape
    per_col = units // chunk
    expand_spec = pl.BlockSpec((row_count, 1, depth, chunk), lambda j: (0, j // per_col, 0, j % per_col))
    shrink_spec = pl.BlockSpec((row_count, 1, chunk, depth), lambda j: (0, j // per_col, j % per_col, 0))
    bias_spec = pl.BlockSpec((1, chunk), lambda j: (0, j))
    return pl.pallas_call(
        mlp_kernel,
        grid=(col_count * per_col,),
        in_specs=[whole(middle.shape), whole(g.shape), expand_spec, bias_spec, shrink_spec, whole(vec.shape)],
        out_specs=[whole(middle.shape), whole(middle.shape), expand_spec, bias_spec, shrink_spec, whole((8, width))],
        out_shape=[
            jax.ShapeDtypeStruct((tokens, width), BF16),
            jax.ShapeDtypeStruct((tokens, width), F32),
            jax.ShapeDtypeStruct(expand.shape, BF16),
            jax.ShapeDtypeStruct(bias.shape, F32),
            jax.ShapeDtypeStruct(shrink.shape, BF16),
            jax.ShapeDtypeStruct((8, width), F32),
        ],
        scratch_shapes=[
            pltpu.VMEM((tokens, width), BF16),
            pltpu.VMEM((tokens, width), F32),
            pltpu.VMEM((tokens, width), F32),
        ],
        compiler_params=params(),
        name="mlp",
    )(middle, g, expand, bias, shrink, vec)


def attend_back(x, dmid, attended, qkv, triple, merge, vec, seq):
    images, rows, width = x.shape
    return pl.pallas_call(
        functools.partial(back_kernel, seq),
        out_shape=[
            jax.ShapeDtypeStruct((images, rows, width), F32),
            jax.ShapeDtypeStruct(triple.shape, BF16),
            jax.ShapeDtypeStruct(merge.shape, BF16),
            jax.ShapeDtypeStruct((8, width), F32),
        ],
        scratch_shapes=[
            pltpu.VMEM((width, 3 * width), BF16),
            pltpu.VMEM((width, width), BF16),
            pltpu.VMEM((images * rows, 3 * width), BF16),
            pltpu.VMEM((images * rows, width), BF16),
            pltpu.VMEM((images * rows, width), BF16),
            pltpu.VMEM((rows, width), BF16),
        ],
        compiler_params=params(),
        name="attend_back",
    )(x, dmid, attended, qkv, triple, merge, vec)


def gather_blocks(block, row_count, col_count):
    half = lax.all_gather(block, "col", axis=0, tiled=False)
    return lax.all_gather(half, "row", axis=0, tiled=False)


def owned_total(blocks):
    mine = lax.psum_scatter(blocks, "row", scatter_dimension=0, tiled=False)
    mine = lax.psum_scatter(mine, "col", scatter_dimension=0, tiled=False)
    return lax.psum(mine, "dp").astype(F32)


def on_device(
    tokens,
    cotangent,
    triple_weight,
    attend_bias,
    merge_weight,
    expand_weight,
    expand_bias,
    shrink_weight,
    norm_gain,
    norm_shift,
    branch_bias,
):
    row_count, col_count = lax.axis_size("row"), lax.axis_size("col")
    images, seq, width = tokens.shape
    rows = -(-seq // 16) * 16
    pad = ((0, 0), (0, rows - seq), (0, 0))
    x = jnp.pad(tokens, pad)
    g = jnp.pad(cotangent, pad).reshape(images * rows, width)
    biases = jnp.concatenate([attend_bias[0], attend_bias[1], expand_bias])
    biases = lax.all_gather(biases, "col", axis=0, tiled=False)
    local = attend_bias.shape[1]
    attend_full = [biases[:, t * local : (t + 1) * local].reshape(1, width) for t in range(2)]
    hidden_bias = biases[:, 2 * local :].reshape(1, -1)
    triple = gather_blocks(triple_weight.transpose(1, 0, 2), row_count, col_count)
    merge = gather_blocks(merge_weight, row_count, col_count)
    expand = gather_blocks(expand_weight, row_count, col_count)
    shrink = gather_blocks(shrink_weight, row_count, col_count)
    filler = jnp.zeros((3, width), F32)
    vec_one = jnp.concatenate([norm_gain[0:1], norm_shift[0:1], branch_bias[0:1]] + attend_full + [filler])
    vec_two = jnp.concatenate([norm_gain[1:2], norm_shift[1:2], branch_bias[1:2], filler, filler[:2]])
    qkv, attended, middle = attend(x, triple, merge, vec_one, seq)
    out, dmid, dexpand, dbias, dshrink, sums_two = mlp(
        middle.reshape(images * rows, width), g, expand, hidden_bias, shrink, vec_two, expand_weight.shape[1] // 3
    )
    dx, dtriple, dmerge, sums_one = attend_back(
        x, dmid.reshape(images, rows, width), attended, qkv, triple, merge, vec_one, seq
    )
    shared = jnp.concatenate([sums_one[0:4], sums_two[0:4], dbias.reshape(-1, width)])
    shared = lax.psum(shared, ("dp", "row", "col"))
    col_at = lax.axis_index("col")
    units = expand_bias.shape[0]
    attend_grad = lax.dynamic_slice_in_dim(shared[2:4], col_at * local, local, 1)
    hidden_grad = lax.dynamic_slice_in_dim(shared[8:].reshape(-1), col_at * units, units, 0)
    return (
        out.reshape(images, rows, width)[:, :seq],
        dx[:, :seq],
        owned_total(dtriple).transpose(1, 0, 2),
        attend_grad,
        owned_total(dmerge),
        owned_total(dexpand),
        hidden_grad,
        owned_total(dshrink),
        jnp.stack([shared[0], shared[4]]),
        jnp.stack([shared[1], shared[5]]),
        shared[6:8],
    )


def solution(mesh):
    placed = (
        P(("dp", "row", "col"), None, None),
        P(("dp", "row", "col"), None, None),
        P("row", None, "col"),
        P(None, "col"),
        P("col", "row"),
        P("row", "col"),
        P("col"),
        P("col", "row"),
        P(),
        P(),
        P(),
    )
    return jax.shard_map(
        on_device,
        mesh=mesh,
        in_specs=placed,
        out_specs=(
            P(("dp", "row", "col"), None, None),
            P(("dp", "row", "col"), None, None),
            P("row", None, "col"),
            P(None, "col"),
            P("col", "row"),
            P("row", "col"),
            P("col"),
            P("col", "row"),
            P(),
            P(),
            P(),
        ),
        check_vma=False,
    )
```

```python
import functools
import math

import jax
import jax.numpy as jnp
from jax import lax
from jax.experimental import pallas as pl
from jax.experimental.pallas import tpu as pltpu
from jax.sharding import PartitionSpec as P

HEAD_DIM = 64
EPSILON = 1e-06
F32 = jnp.float32
BF16 = jnp.bfloat16
VMEM_BYTES = 56 * 1024 * 1024


def mean_rows(source):
    return jnp.mean(source, axis=-1, keepdims=True)


def unit_norm(source):
    average = mean_rows(source)
    variance = mean_rows(source * source) - average * average
    inverse = lax.rsqrt(variance + EPSILON)
    return (source - average) * inverse, inverse


def norm_backward(grad, unit, inverse, gain):
    scaled = grad * gain
    return inverse * (scaled - mean_rows(scaled) - unit * mean_rows(scaled * unit))


def dot(left, right):
    return jnp.dot(left, right, preferred_element_type=F32)


def dot_rows(left, right):
    return lax.dot_general(left, right, (((1,), (1,)), ((), ())), preferred_element_type=F32)


def dot_tokens(left, right):
    return lax.dot_general(left, right, (((0,), (0,)), ((), ())), preferred_element_type=F32)


def column_sum(source):
    return jnp.sum(source, axis=0, keepdims=True)


def assemble(block_refs, triple_full, merge_full):
    depth = block_refs[0].shape[1]
    width = 2 * depth
    for r in range(2):
        for c in range(2):
            block = block_refs[2 * r + c]
            for t in range(3):
                triple_full[r * depth : (r + 1) * depth, t * width + c * depth : t * width + (c + 1) * depth] = (
                    block[t * depth : (t + 1) * depth]
                )
            merge_full[c * depth : (c + 1) * depth, r * depth : (r + 1) * depth] = block[3 * depth : 4 * depth]


def attend_kernel(seq, x_ref, own, across, twin, twin_across, vec_ref, qkv_ref, attended_ref, middle_ref, triple_full, merge_full):
    width = x_ref.shape[-1]
    rows = x_ref.shape[1]

    @pl.when(pl.program_id(0) == 0)
    def _():
        assemble((own, across, twin, twin_across), triple_full, merge_full)

    x = x_ref[0].astype(F32)
    unit, _ = unit_norm(x)
    normed = (unit * vec_ref[0:1] + vec_ref[1:2]).astype(BF16)
    qkv_ref[0, :, 0:width] = (dot(normed, triple_full[:, 0:width]) + vec_ref[3:4]).astype(BF16)
    qkv_ref[0, :, width : 2 * width] = dot(normed, triple_full[:, width : 2 * width]).astype(BF16)
    qkv_ref[0, :, 2 * width : 3 * width] = (
        dot(normed, triple_full[:, 2 * width : 3 * width]) + vec_ref[4:5]
    ).astype(BF16)
    pair = 2 * HEAD_DIM
    first = lax.broadcasted_iota(jnp.int32, (rows, pair), 1) < HEAD_DIM
    live = lax.broadcasted_iota(jnp.int32, (rows, rows), 1) < seq
    scale = HEAD_DIM**-0.5
    zero = jnp.zeros((rows, pair), BF16)
    for p in range(width // pair):
        q = qkv_ref[0, :, p * pair : (p + 1) * pair]
        k = qkv_ref[0, :, width + p * pair : width + (p + 1) * pair]
        v = qkv_ref[0, :, 2 * width + p * pair : 2 * width + (p + 1) * pair]
        outs = []
        for h in range(2):
            mine = first if h == 0 else jnp.logical_not(first)
            logits = dot_rows(jnp.where(mine, q, zero), k) * scale
            logits = jnp.where(live, logits, -1e30)
            top = jnp.max(logits, axis=-1, keepdims=True)
            powers = jnp.exp(logits - top)
            probs = powers * (1.0 / jnp.sum(powers, axis=-1, keepdims=True))
            outs.append(dot(probs.astype(BF16), v))
        attended_ref[0, :, p * pair : (p + 1) * pair] = jnp.where(first, outs[0], outs[1]).astype(BF16)
    middle_ref[0] = x + dot(attended_ref[0], merge_full[...]) + vec_ref[2:3]


def mlp_kernel(final, middle_ref, g_ref, e0, e1, bias_ref, s0, s1, vec_ref, *refs):
    if final:
        acc_in, back_in, out_ref, dmid_ref, dexpand_ref, dbias_ref, dshrink_ref, sums_ref, normed_ref, acc_ref, back_ref = refs
    else:
        acc_ref, back_ref, dexpand_ref, dbias_ref, dshrink_ref, normed_ref = refs
    step = pl.program_id(0)

    @pl.when(step == 0)
    def _():
        unit, _ = unit_norm(middle_ref[...])
        normed_ref[...] = (unit * vec_ref[0:1] + vec_ref[1:2]).astype(BF16)
        if final:
            acc_ref[...] = acc_in[...]
            back_ref[...] = back_in[...]
        else:
            acc_ref[...] = jnp.zeros_like(acc_ref)
            back_ref[...] = jnp.zeros_like(back_ref)

    expand = jnp.concatenate([e0[...], e1[...]], axis=0)
    shrink = jnp.concatenate([s0[...], s1[...]], axis=1)
    normed = normed_ref[...]
    g = g_ref[...]
    hidden = dot(normed, expand) + bias_ref[...]
    cdf = 0.5 * (1.0 + lax.erf(hidden * (0.5**0.5)))
    slope = cdf + hidden * (jnp.exp(-0.5 * hidden * hidden) * (1.0 / math.sqrt(2.0 * math.pi)))
    active = (hidden * cdf).astype(BF16)
    acc_ref[...] += dot(active, shrink)
    dhidden = (dot_rows(g, shrink) * slope).astype(BF16)
    dbias_ref[...] = column_sum(dhidden.astype(F32))
    back_ref[...] += dot_rows(dhidden, expand)
    dshrink = dot_tokens(active, g).astype(BF16)
    dexpand = dot_tokens(dhidden, normed).astype(BF16)
    cols = dshrink.shape[1] // 2
    for r in range(2):
        dshrink_ref[r] = dshrink[:, r * cols : (r + 1) * cols]
        dexpand_ref[r] = dexpand[:, r * cols : (r + 1) * cols]

    if final:

        @pl.when(step == pl.num_programs(0) - 1)
        def _():
            middle = middle_ref[...]
            out_ref[...] = (middle + acc_ref[...] + vec_ref[2:3]).astype(BF16)
            unit, inverse = unit_norm(middle)
            wide = g_ref[...].astype(F32)
            back = back_ref[...]
            dmid = wide + norm_backward(back, unit, inverse, vec_ref[0:1])
            dmid_ref[...] = dmid
            sums_ref[0:1] = column_sum(back * unit)
            sums_ref[1:2] = column_sum(back)
            sums_ref[2:3] = column_sum(dmid)
            sums_ref[3:4] = column_sum(wide)


def back_kernel(
    seq, x_ref, dmid_ref, qkv_ref, own, across, twin, twin_across, vec_ref,
    dx_ref, dqkv_ref, normed_ref, sums_ref,
    triple_full, merge_full, datt_ref,
):
    images, rows, width = x_ref.shape
    assemble((own, across, twin, twin_across), triple_full, merge_full)
    pair = 2 * HEAD_DIM
    scale = HEAD_DIM**-0.5
    sums_ref[...] = jnp.zeros_like(sums_ref)

    @pl.loop(0, images)
    def _(image):
        x = x_ref[image].astype(F32)
        unit, inverse = unit_norm(x)
        normed_ref[image] = (unit * vec_ref[0:1] + vec_ref[1:2]).astype(BF16)
        dmid = dmid_ref[image]
        g1 = dmid.astype(BF16)
        datt_ref[...] = dot_rows(g1, merge_full[...]).astype(BF16)
        first = lax.broadcasted_iota(jnp.int32, (rows, pair), 1) < HEAD_DIM
        live = lax.broadcasted_iota(jnp.int32, (rows, rows), 0) < seq
        zero = jnp.zeros((rows, pair), BF16)
        for p in range(width // pair):
            q = qkv_ref[image, :, p * pair : (p + 1) * pair]
            k = qkv_ref[image, :, width + p * pair : width + (p + 1) * pair]
            v = qkv_ref[image, :, 2 * width + p * pair : 2 * width + (p + 1) * pair]
            da = datt_ref[:, p * pair : (p + 1) * pair]
            dq, dk, dv = [], [], []
            for h in range(2):
                mine = first if h == 0 else jnp.logical_not(first)
                logits = dot_rows(k, jnp.where(mine, q, zero)) * scale
                logits = jnp.where(live, logits, -1e30)
                top = jnp.max(logits, axis=0, keepdims=True)
                powers = jnp.exp(logits - top)
                probs = powers * (1.0 / column_sum(powers))
                dprobs = dot_rows(v, jnp.where(mine, da, zero))
                weighted = probs * dprobs
                dlogits = ((weighted - probs * column_sum(weighted)) * scale).astype(BF16)
                dq.append(dot_tokens(dlogits, k))
                dk.append(dot(dlogits, q))
                dv.append(dot(probs.astype(BF16), da))
            for t, parts in enumerate((dq, dk, dv)):
                dqkv_ref[image, :, t * width + p * pair : t * width + (p + 1) * pair] = jnp.where(
                    first, parts[0], parts[1]
                ).astype(BF16)
        dnormed = dot_rows(dqkv_ref[image], triple_full[...])
        dx_ref[image] = dmid + norm_backward(dnormed, unit, inverse, vec_ref[0:1])
        sums_ref[0:1] += column_sum(dnormed * unit)
        sums_ref[1:2] += column_sum(dnormed)
        sums_ref[2:3] += column_sum(dqkv_ref[image, :, 0:width].astype(F32))
        sums_ref[3:4] += column_sum(dqkv_ref[image, :, 2 * width : 3 * width].astype(F32))


def weights_kernel(
    count, *refs,
):
    normed_refs, dqkv_refs = refs[:count], refs[count : 2 * count]
    attended_ref, dmid_ref, dfirst_ref, dsecond_ref = refs[2 * count :]
    width = attended_ref.shape[-1]
    depth = cols = width // 2

    def tall(parts):
        return parts.reshape(parts.shape[0] * parts.shape[1], parts.shape[2])

    normed = jnp.concatenate([tall(ref[...]) for ref in normed_refs], axis=0)
    for c in range(2):
        for t in range(3):
            at = t * width + c * cols
            grads = jnp.concatenate([tall(ref[:, :, at : at + cols]) for ref in dqkv_refs], axis=0)
            part = dot_tokens(normed, grads).astype(BF16)
            for r in range(2):
                home = dfirst_ref if t < 2 else dsecond_ref
                home[r, c, t % 2 * depth : (t % 2 + 1) * depth] = part[r * depth : (r + 1) * depth]

    attended = tall(attended_ref[...])
    for r in range(2):
        part = dot_tokens(attended, tall(dmid_ref[:, :, r * cols : (r + 1) * cols]).astype(BF16)).astype(BF16)
        for c in range(2):
            dsecond_ref[r, c, depth : 2 * depth] = part[c * depth : (c + 1) * depth]


def whole(shape):
    return pl.BlockSpec(shape, lambda *_: (0,) * len(shape))


def per_image(shape):
    return pl.BlockSpec((1,) + shape, lambda i: (i, 0, 0))


def params():
    return pltpu.CompilerParams(vmem_limit_bytes=VMEM_BYTES)


def cost(flops):
    return pl.CostEstimate(flops=2 * flops, bytes_accessed=20_000_000, transcendentals=2_000_000)


def attend(x, blocks, vec, seq):
    images, rows, width = x.shape
    return pl.pallas_call(
        functools.partial(attend_kernel, seq),
        grid=(images,),
        in_specs=[per_image((rows, width))] + [whole(block.shape) for block in blocks] + [whole(vec.shape)],
        out_specs=[per_image((rows, 3 * width)), per_image((rows, width)), per_image((rows, width))],
        out_shape=[
            jax.ShapeDtypeStruct((images, rows, 3 * width), BF16),
            jax.ShapeDtypeStruct((images, rows, width), BF16),
            jax.ShapeDtypeStruct((images, rows, width), F32),
        ],
        scratch_shapes=[pltpu.VMEM((width, 3 * width), BF16), pltpu.VMEM((width, width), BF16)],
        compiler_params=params(),
        cost_estimate=cost(2 * images * rows * width * (4 * width + 4 * rows)),
        name="attend",
    )(x, *blocks, vec)


def mlp(middle, g, expand, bias, shrink, vec, chunk, carried=None):
    tokens, width = middle.shape
    depth, units = expand[0].shape
    tall = whole(middle.shape)
    expand_specs = [pl.BlockSpec((depth, chunk), lambda j: (0, j))] * 2
    shrink_specs = [pl.BlockSpec((chunk, depth), lambda j: (j, 0))] * 2
    grad_spec = pl.BlockSpec((2, chunk, depth), lambda j: (0, j, 0))
    bias_spec = pl.BlockSpec((1, chunk), lambda j: (0, j))
    grad_shape = jax.ShapeDtypeStruct((2, units, depth), BF16)
    wide = jax.ShapeDtypeStruct((tokens, width), F32)
    grads = [grad_shape, jax.ShapeDtypeStruct(bias.shape, F32), grad_shape]
    grad_specs = [grad_spec, bias_spec, grad_spec]
    scratch = [pltpu.VMEM((tokens, width), BF16)]
    if carried is None:
        carried = ()
        out_specs, out_shape = [tall, tall] + grad_specs, [wide, wide] + grads
    else:
        out_specs = [tall, tall] + grad_specs + [whole((8, width))]
        out_shape = [jax.ShapeDtypeStruct((tokens, width), BF16), wide] + grads + [jax.ShapeDtypeStruct((8, width), F32)]
        scratch = scratch + [pltpu.VMEM((tokens, width), F32)] * 2
    return pl.pallas_call(
        functools.partial(mlp_kernel, len(carried) > 0),
        grid=(units // chunk,),
        in_specs=[tall, tall] + expand_specs + [bias_spec] + shrink_specs + [whole(vec.shape)] + [tall] * len(carried),
        out_specs=out_specs,
        out_shape=out_shape,
        scratch_shapes=scratch,
        compiler_params=params(),
        cost_estimate=cost(12 * tokens * width * units),
        name="mlp",
    )(middle, g, *expand, bias, *shrink, vec, *carried)


def attend_back(x, dmid, qkv, blocks, vec, seq, start, images):
    _, rows, width = x.shape

    def part(last):
        return pl.BlockSpec((images, rows, last), lambda i: (start // images, 0, 0))

    return pl.pallas_call(
        functools.partial(back_kernel, seq),
        grid=(1,),
        in_specs=[part(width), part(width), part(3 * width)] + [whole(block.shape) for block in blocks] + [whole(vec.shape)],
        out_specs=[
            whole((images, rows, width)),
            whole((images, rows, 3 * width)),
            whole((images, rows, width)),
            whole((8, width)),
        ],
        out_shape=[
            jax.ShapeDtypeStruct((images, rows, width), F32),
            jax.ShapeDtypeStruct((images, rows, 3 * width), BF16),
            jax.ShapeDtypeStruct((images, rows, width), BF16),
            jax.ShapeDtypeStruct((8, width), F32),
        ],
        scratch_shapes=[
            pltpu.VMEM((width, 3 * width), BF16),
            pltpu.VMEM((width, width), BF16),
            pltpu.VMEM((rows, width), BF16),
        ],
        compiler_params=params(),
        cost_estimate=cost(2 * images * rows * width * (4 * width + 10 * rows)),
        name="attend_back",
    )(x, dmid, qkv, *blocks, vec)


def attend_weights(normed, dqkv, attended, dmid):
    images, rows, width = attended.shape
    return pl.pallas_call(
        functools.partial(weights_kernel, len(normed)),
        out_shape=[jax.ShapeDtypeStruct((2, 2, width, width // 2), BF16)] * 2,
        compiler_params=params(),
        cost_estimate=cost(2 * images * rows * width * 4 * width),
        name="attend_weights",
    )(*normed, *dqkv, attended, dmid)


def swap(source, axis, bit=0):
    count = lax.axis_size(axis)
    return lax.ppermute(source, axis, [(i, i ^ (1 << bit)) for i in range(count)])


def half_of(source, which, dim=0):
    size = source.shape[dim] // 2
    return lax.dynamic_slice_in_dim(source, which * size, size, dim)


def side(bit):
    return (lax.axis_index("dp") >> bit) & 1


def ordered(mine, other, which, dim=0):
    return jnp.where(
        which == 0, jnp.concatenate([mine, other], dim), jnp.concatenate([other, mine], dim)
    )


def together(chains, outputs=()):
    received, counts = [], []
    for chain in chains:
        sends = chain["sends"]
        counts.append(len(sends))
        received += [swap(*send) for send in sends]
    flat, tree = jax.tree.flatten(outputs)
    held = lax.optimization_barrier(tuple(received) + tuple(flat))
    received, outputs = list(held[: len(received)]), jax.tree.unflatten(tree, held[len(received) :])
    for chain, count in zip(chains, counts):
        mine, received = received[:count], received[count:]
        advance(chain, mine)
    return outputs


def alternate(here, there):
    flying = [[swap(*send) for send in chain["sends"]] for chain in there]
    while any(chain["sends"] for chain in here + there):
        started = [[swap(*send) for send in chain["sends"]] for chain in here]
        ready = [[send[0] for send in chain["sends"]] for chain in here]
        flying, _ = lax.optimization_barrier((flying, ready))
        for chain, received in zip(there, flying):
            if received:
                advance(chain, received)
        here, there, flying = there, here, started


def begin(steps):
    chain = {"steps": steps, "sends": None, "result": None}
    chain["sends"] = next(steps)
    return chain


def advance(chain, received):
    try:
        chain["sends"] = chain["steps"].send(received)
    except StopIteration as stop:
        chain["sends"], chain["result"] = [], stop.value


def bit_count():
    return lax.axis_size("dp").bit_length() - 1


def gather_steps(block):
    if bit_count() > 0:
        at = side(0)
        mine, twin = yield [(half_of(block, at), "col"), (block, "row")]
        (other,) = yield [(mine, "dp")]
        across = ordered(mine, other, at)
    else:
        across, twin = yield [(block, "col"), (block, "row")]
    (twin_across,) = yield [(across, "row")]
    return block, across, twin, twin_across


def sum_steps(parts, col_first):
    total = []
    while len(total) < 2:
        fresh = parts[len(total) :]
        received = yield [(part[1], "row") for part in fresh]
        total += [part[0].astype(F32) + got.astype(F32) for part, got in zip(fresh, received)]
    bits = bit_count()
    order = list(range(bits))
    order.insert(0 if col_first else min(1, bits), "col")
    for bit in order:
        if bit == "col":
            (got,) = yield [(total[1].astype(BF16), "col")]
            total = [total[0] + got.astype(F32)]
        else:
            received = yield [(half_of(one, 1 - side(bit)).astype(BF16), "dp", bit) for one in total]
            total = [half_of(one, side(bit)) + got.astype(F32) for one, got in zip(total, received)]
    total = total[0].astype(BF16)
    for bit in reversed(range(bits)):
        (got,) = yield [(total, "dp", bit)]
        total = ordered(total, got, side(bit))
    return total.astype(F32)


def everywhere_steps(source):
    for axis in ("row", "col"):
        (got,) = yield [(source, axis)]
        source = source + got
    for bit in range(bit_count()):
        (got,) = yield [(source, "dp", bit)]
        source = source + got
    return source


def on_device(
    tokens,
    cotangent,
    triple_weight,
    attend_bias,
    merge_weight,
    expand_weight,
    expand_bias,
    shrink_weight,
    norm_gain,
    norm_shift,
    branch_bias,
):
    images, seq, width = tokens.shape
    rows = -(-seq // 16) * 16
    row_at, col_at = lax.axis_index("row"), lax.axis_index("col")

    def turn(source):
        cut = source.shape[-1] // 2
        return ordered(source[..., :cut], source[..., cut:], row_at, source.ndim - 1)

    pad = ((0, 0), (0, rows - seq), (0, 0))
    x = jnp.pad(turn(tokens), pad)
    g = jnp.pad(turn(cotangent), pad).reshape(images * rows, width)
    biases = jnp.concatenate([attend_bias[0], attend_bias[1], expand_bias]).reshape(1, -1)
    biases = jnp.concatenate([biases, swap(biases, "col")])
    local = attend_bias.shape[1]
    attend_full = [biases[:, t * local : (t + 1) * local].reshape(1, width) for t in range(2)]
    hidden_bias = biases[:, 2 * local :]
    attention = begin(gather_steps(
        jnp.concatenate([triple_weight.transpose(1, 0, 2), merge_weight[None]]).reshape(4 * local, local)
    ))
    x, g, biases = together([attention], (x, g, biases))
    late_expand, late_shrink = lax.optimization_barrier((expand_weight, shrink_weight, attention["sends"][0][0]))[:2]
    late = [begin(gather_steps(late_expand)), begin(gather_steps(late_shrink))]
    pending = [[swap(*send) for send in chain["sends"]] for chain in late]
    while attention["result"] is None:
        together([attention])
    attention = attention["result"]
    filler = jnp.zeros((3, width), F32)
    gain, shift, branch = turn(norm_gain), turn(norm_shift), turn(branch_bias)
    vec_one = jnp.concatenate([gain[0:1], shift[0:1], branch[0:1]] + attend_full + [filler])
    vec_two = jnp.concatenate([gain[1:2], shift[1:2], branch[1:2], filler, filler[:2]])
    pending, (qkv, attended, middle) = lax.optimization_barrier(
        (pending, tuple(attend(x, attention, vec_one, seq)))
    )
    for chain, received in zip(late, pending):
        advance(chain, received)
    middle = middle.reshape(images * rows, width)
    units = expand_bias.shape[0]
    chunk = units // 3
    acc, back, dexpand, dbias, dshrink = together(
        late,
        tuple(mlp(middle, g, (expand_weight, pending[0][1]), hidden_bias[0:1], (shrink_weight, pending[1][1]), vec_two, chunk)),
    )
    while late[0]["result"] is None:
        together(late)
    expand, shrink = late[0]["result"], late[1]["result"]
    sums = [[dshrink], [dexpand]]
    chains = [begin(sum_steps(sums[0], True)), begin(sum_steps(sums[1], False))]
    out, dmid, dexpand, dbias_far, dshrink, sums_two = mlp(
        middle, g, (expand[1], expand[3]), hidden_bias[1:2], (shrink[1], shrink[3]), vec_two, chunk, (acc, back)
    )
    sums[0].append(dshrink)
    sums[1].append(dexpand)
    out, dmid, dbias_far, sums_two = together(chains, (out, dmid, dbias_far, sums_two))
    dmid = dmid.reshape(images, rows, width)
    pieces = 2 if images % 2 == 0 else 1
    count = images // pieces
    done = []
    for piece in range(pieces):
        done.append(together(chains, tuple(attend_back(x, dmid, qkv, attention, vec_one, seq, piece * count, count))))
    dx = jnp.concatenate([held[0] for held in done])
    sums_one = sum(held[3] for held in done)
    dfirst, dsecond = together(
        chains, tuple(attend_weights([held[2] for held in done], [held[1] for held in done], attended, dmid))
    )
    dbias = ordered(dbias, dbias_far, col_at, 1).reshape(-1, width)
    dattend = ordered(sums_one[2:4, :local], sums_one[2:4, local:], col_at, 1)
    shared = jnp.concatenate([turn(sums_one[0:2]), dattend, turn(sums_two[0:4]), dbias])
    chains += [
        begin(sum_steps([dfirst[:, 0], dfirst[:, 1]], True)),
        begin(sum_steps([dsecond[:, 0], dsecond[:, 1]], False)),
        begin(everywhere_steps(shared)),
    ]
    alternate(chains[2:4], chains[0:2] + chains[4:])
    shrink_grad, expand_grad, first, second, shared = [chain["result"] for chain in chains]
    expand_grad = expand_grad.T
    first, second = first.reshape(2, local, local), second.reshape(2, local, local)
    attend_grad = lax.dynamic_slice_in_dim(shared[2:4], col_at * local, local, 1)
    hidden_grad = lax.dynamic_slice_in_dim(shared[8:].reshape(-1), col_at * units, units, 0)
    return (
        turn(out.reshape(images, rows, width)[:, :seq]),
        turn(dx[:, :seq]),
        jnp.stack([first[0], first[1], second[0]], axis=1),
        attend_grad,
        second[1],
        expand_grad,
        hidden_grad,
        shrink_grad,
        jnp.stack([shared[0], shared[4]]),
        jnp.stack([shared[1], shared[5]]),
        shared[6:8],
    )


def solution(mesh):
    placed = (
        P(("dp", "row", "col"), None, None),
        P(("dp", "row", "col"), None, None),
        P("row", None, "col"),
        P(None, "col"),
        P("col", "row"),
        P("row", "col"),
        P("col"),
        P("col", "row"),
        P(),
        P(),
        P(),
    )
    return jax.shard_map(
        on_device,
        mesh=mesh,
        in_specs=placed,
        out_specs=(
            P(("dp", "row", "col"), None, None),
            P(("dp", "row", "col"), None, None),
            P("row", None, "col"),
            P(None, "col"),
            P("col", "row"),
            P("row", "col"),
            P("col"),
            P("col", "row"),
            P(),
            P(),
            P(),
        ),
        check_vma=False,
    )
```
